256 devices in a mesh: group: 16 (over z, x_lo), section: 2 (over x_hi), tensor: 8 (over y, core).
Axes of the slice: x: 4 (x_hi: 2, x_lo: 2; x = x_hi * 2 + x_lo), y: 4, z: 8, core: 2. Of those that a mesh axis runs over, the one named last changes fastest.
Arguments:
- prompt_tokens: bfloat16 [512, 128, 8192], P(('group', 'section'), None, 'tensor'), may hold values from -6 to 6
- kv_weight: bfloat16 [8192, 2048], P('tensor'), may hold values from -0.0625 to 0.0625
- routes: int32 [512, 1], replicated, may hold values from 0 to 15; in each aligned block of 16 rows (0 to 15, 16 to 31, ...) at most 2 rows name the same one
- lengths: int32 [512], replicated, may hold values from 1 to 128, 40960 in all
- queries: bfloat16 [16, 2, 16, 2, 4, 8192], P('group', 'section', None, None, None, 'tensor'), may hold values from -6 to 6
- new_kv: bfloat16 [16, 2, 16, 2, 4, 2048], P('group', 'section', None, None, None, 'tensor'), may hold values from -6 to 6
Outputs:
- decode_cache: bfloat16 [16, 2, 16, 2, 2048, 128], P('group', 'section', None, None, 'tensor')
- attention: bfloat16 [16, 2, 16, 2, 4, 8192], P('group', 'section', None, None, None, 'tensor')
The draws below stay inside these ranges and needn't reach their ends.
Inputs may be any that keep to these rules, and one draw needn't show every extreme that they name: `routes`: in each block of 16 prompts (those of one group and section index) no decode group is named more than 2 times, and some block names one group exactly 2 times.
All inputs are finite; a program needn't handle non-finite values.
Results may differ from the reference program's by a relative error of at most 0.017.
Values may be sent and summed in bfloat16 or wider, within the bound.
No kernel may reach another device: no remote copies, remote signals or barrier semaphores. Data moves between devices by JAX's collectives and lax.ppermute only.
A program may use at most 64 MiB of HBM per device.

```python
import math
import jax
import jax.numpy as jnp
import numpy as np
from jax import lax

D = 8192
HEADS = 64
KV_HEADS = 8
HD = 128
CAP = 2
STEPS = 4
PLEN = 128
PR = 16
PROMPTS = 512
N_GROUP = 16
N_SECTION = 2
N_TENSOR = 8


def shared_plan(key):
    sign_key, plant_key, query_key, size_key = jax.random.split(key, 4)
    leading = (N_GROUP, N_SECTION, N_GROUP, CAP, KV_HEADS)
    direction = jnp.where(jax.random.bernoulli(sign_key, 0.5, leading + (HD,)), 1.0, -1.0).astype(jnp.float32)
    planted = jax.random.bernoulli(plant_key, 0.25, leading)
    query_size = jax.random.uniform(query_key, leading, jnp.float32, 3.5, 5.5)
    key_size = jax.random.uniform(size_key, leading, jnp.float32, 3.5, 5.5)
    return (direction, planted, query_size, key_size)


def draw_queries(key, part):
    direction, planted, query_size, unused = shared_plan(key)
    key = jax.random.fold_in(key, 11)
    per_group = HEADS // KV_HEADS
    background = jax.random.truncated_normal(key, -6.0, 6.0, (N_GROUP, N_SECTION, N_GROUP, CAP, STEPS, KV_HEADS, per_group, HD), jnp.float32)
    aligned = (query_size[..., None] * direction)[:, :, :, :, None, :, None, :]
    use_mask = planted[:, :, :, :, None, :, None, None]
    drawn = jnp.where(use_mask, aligned, background)
    return drawn.reshape(N_GROUP, N_SECTION, N_GROUP, CAP, STEPS, HEADS * HD).astype(jnp.bfloat16)


def draw_new_kv(key, part):
    direction, planted, unused, key_size = shared_plan(key)
    key = jax.random.fold_in(key, 23)
    background = jax.random.truncated_normal(key, -6.0, 6.0, (N_GROUP, N_SECTION, N_GROUP, CAP, STEPS, KV_HEADS, 2, HD), jnp.float32)
    leading_key = key_size[..., None] * direction
    entry_ids = jnp.arange(HD)
    trimmed = jnp.where(entry_ids == 0, 0.0, leading_key)
    step_ids = jnp.arange(STEPS)
    aligned = jnp.where((step_ids == 0)[:, None, None], leading_key[:, :, :, :, None], trimmed[:, :, :, :, None])
    use_mask = jnp.logical_and(planted[:, :, :, :, None, :, None], (step_ids < 2)[:, None, None])
    key_rows = jnp.where(use_mask, aligned, background[..., 0, :])
    drawn = jnp.stack([key_rows, background[..., 1, :]], axis=-2)
    return drawn.reshape(N_GROUP, N_SECTION, N_GROUP, CAP, STEPS, 2 * KV_HEADS * HD).astype(jnp.bfloat16)


def levels(own_key, dims, cuts, least, top_value):
    def one(axis_at, parts):
        draws = jax.random.uniform(jax.random.fold_in(jax.random.fold_in(own_key, 6), axis_at), (parts,), jnp.float32, least / len(cuts), top_value / len(cuts))
        return jnp.repeat(jnp.exp(draws), dims[axis_at] // parts).reshape((-1,) + (1,) * (len(dims) - axis_at - 1))

    loudness = one(*cuts[0])
    for cut in cuts[1:]:
        loudness = loudness * one(*cut)
    return loudness


def profile(count, total, limit, slope):
    weights = [(1 << 20) // math.isqrt(grade ** slope) + 1 for grade in range(2, count + 1)]
    spare, counts = total - limit - (count - 1), [1] * (count - 1)
    while spare > 0:
        candidates = [i for i in range(count - 1) if counts[i] < limit]
        mass, budget = sum([weights[i] for i in candidates]), spare
        for i in candidates:
            more = min(limit - counts[i], max(1, budget * weights[i] // mass), spare)
            counts[i] = counts[i] + more
            spare = spare - more
    return np.array([limit] + counts)


def uneven(rng, amount, total, most, lean):
    if amount == 2:
        one = jax.random.randint(rng, (), max(1, total - most), min(most, total - 1) + 1)
        return jnp.stack([one, total - one])
    sizes = jnp.asarray(profile(amount, total, most, lean), jnp.int32)
    pairs = (amount - 1) // 2
    source_of, taker = sizes[1:1 + 2 * pairs:2], sizes[2:2 + 2 * pairs:2]
    margin = jnp.minimum(source_of - 1, most - taker)
    passed = jax.random.randint(jax.random.fold_in(rng, 1), (pairs,), 0, 1 << 20) % (margin + 1)
    sizes = sizes.at[1:1 + 2 * pairs:2].set(source_of - passed).at[2:2 + 2 * pairs:2].set(taker + passed)
    return sizes[jax.random.permutation(jax.random.fold_in(rng, 2), amount)]


def shared_out(own_key, own, number, rows, amount, top, limit, lean):
    ranking = jax.random.permutation(own_key, amount)
    heavy_load, common = load_shares(amount, rows * top, limit, lean, True), load_shares(amount, rows * top, limit, lean, False)
    places = jnp.arange(amount)

    def named(tallies, offset_by):
        used = int((tallies > 0).sum())
        fixed = max(1, used // 4)
        shifted = fixed + (places - fixed + offset_by * (used - fixed)) % max(1, amount - fixed)
        return jnp.zeros((amount,), jnp.int32).at[ranking[jnp.where(places < fixed, places, shifted)]].set(jnp.asarray(tallies, jnp.int32))

    tallies = jnp.where(number % 4 == 0, named(heavy_load, number // 4), named(common, number - number // 4 - 1))
    mixed = jax.random.permutation(jax.random.fold_in(own, 3), amount)
    donor, sink = mixed[0:amount // 2 * 2:2], mixed[1:amount // 2 * 2:2]
    slack = jnp.minimum(tallies[donor] - 1, limit - tallies[sink]) // 2
    slack = jnp.where((donor == ranking[0]) | (sink == ranking[0]) | (tallies[sink] == 0), 0, jnp.maximum(slack, 0))
    shifted = jax.random.randint(jax.random.fold_in(own, 4), (amount // 2,), 0, 1 << 20) % (slack + 1)
    tallies = tallies.at[donor].add(-shifted).at[sink].add(shifted)
    items = jnp.searchsorted(jnp.cumsum(tallies), jnp.arange(rows * top), side="right").astype(jnp.int32)
    listing = items.reshape(top, rows).T
    listing = listing[jax.random.permutation(jax.random.fold_in(own, 1), rows)]
    offset_by = jax.random.randint(jax.random.fold_in(own, 2), (rows, 1), 0, top)
    return jnp.take_along_axis(listing, (jnp.arange(top)[None, :] + offset_by) % top, axis=1)


def load_shares(amount, total, reach, skew, full):
    weights = [(1 << 20) // math.isqrt(standing ** skew) + 1 for standing in range(1, amount + 1)]
    largest = reach if full else min(reach, max(-(-total // amount), total * weights[0] // sum(weights)))
    least = 1 if total - largest >= amount - 1 else 0
    holding, surplus = [largest] + [least] * (amount - 1), total - largest - least * (amount - 1)
    while surplus > 0:
        candidates = [i for i in range(1, amount) if holding[i] < largest] or [i for i in range(1, amount) if holding[i] < reach]
        pool, remaining = sum([weights[i] for i in candidates]), surplus
        for i in candidates:
            more = min(reach - holding[i], max(1, remaining * weights[i] // pool), surplus)
            holding[i] = holding[i] + more
            surplus = surplus - more
    return np.array(holding)


def scatter_about(rng, shape, deviation, limit, cuts=(), kind=jnp.bfloat16):
    result = deviation * jax.random.normal(rng, shape, jnp.float32)
    if cuts:
        result = result * levels(rng, shape, cuts, -0.22, 0.18)
    return jnp.clip(result, -limit, limit).astype(kind)


def setup_inputs(seed: int = 0) -> dict:
    key_list = jax.random.split(jax.random.key(seed), 7)
    prompt_tokens = scatter_about(key_list[0], (PROMPTS, PLEN, D), 1.0, 6.0, ((0, 32), (2, 8)))
    kv_weight = scatter_about(key_list[1], (D, 2 * KV_HEADS * HD), D ** -0.5, 0.0625, ((0, 8),))
    routes_keys = jax.random.split(jax.random.fold_in(key_list[2], 1), PROMPTS // PR)
    routes_turns = jax.random.permutation(jax.random.fold_in(key_list[2], 3), PROMPTS // PR)
    routes = jax.vmap(lambda own, number: shared_out(jax.random.fold_in(key_list[2], 2), own, number, PR, N_GROUP, 1, CAP, 2))(routes_keys, routes_turns).reshape((PROMPTS, 1))
    lengths = uneven(key_list[3], PROMPTS, PROMPTS * PLEN * 5 // 8, PLEN, 1).astype(jnp.int32)
    queries = draw_queries(jax.random.fold_in(key_list[6], 71), 0)
    new_kv = draw_new_kv(jax.random.fold_in(key_list[6], 71), 0)
    return {"prompt_tokens": prompt_tokens, "kv_weight": kv_weight, "routes": routes, "lengths": lengths, "queries": queries, "new_kv": new_kv}


neg_big = -1.0e30


def slot_ranks(route_rows):
    row_count = route_rows.shape[-1]
    order_ids = jnp.arange(row_count, dtype=jnp.int32)
    earlier = order_ids[:, None] > order_ids[None, :]
    same_route = route_rows[..., :, None] == route_rows[..., None, :]
    return jnp.sum(jnp.logical_and(same_route, earlier), axis=-1).astype(jnp.int32)


def attend(query_f, key_f, value_f, live_rows, fresh_keys, fresh_vals):
    factor = HD ** -0.5
    old_scores = jnp.einsum("scjhgd,schdl->scjhgl", query_f, key_f) * factor
    old_scores = jnp.where(live_rows[:, :, None, None, None, :], old_scores, neg_big)
    new_scores = jnp.einsum("scjhgd,scihd->scjhgi", query_f, fresh_keys) * factor
    step_count = new_scores.shape[-1]
    causal = jnp.arange(step_count)[None, :] <= jnp.arange(step_count)[:, None]
    new_scores = jnp.where(causal[None, None, :, None, None, :], new_scores, neg_big)
    top_score = jnp.maximum(jnp.max(old_scores, axis=-1), jnp.max(new_scores, axis=-1))
    old_weights = jnp.exp(old_scores - top_score[..., None])
    new_weights = jnp.exp(new_scores - top_score[..., None])
    weight_total = jnp.sum(old_weights, axis=-1) + jnp.sum(new_weights, axis=-1)
    old_round = lax.optimization_barrier(old_weights.astype(jnp.bfloat16)).astype(jnp.float32)
    new_round = lax.optimization_barrier(new_weights.astype(jnp.bfloat16)).astype(jnp.float32)
    summed = jnp.einsum("scjhgl,schdl->scjhgd", old_round, value_f) + jnp.einsum("scjhgi,scihd->scjhgd", new_round, fresh_vals)
    return summed / weight_total[..., None]


def reference(prompt_tokens, kv_weight, routes, lengths, queries, new_kv):
    per_group = HEADS // KV_HEADS
    columns = 2 * KV_HEADS * HD
    pair_count = N_GROUP * N_SECTION
    feat_block = D // N_TENSOR
    weight_parts = kv_weight.reshape(N_TENSOR, feat_block, columns)

    def project(bundle):
        prompt_block, block_lengths = bundle
        token_parts = jnp.swapaxes(prompt_block.reshape(PR * PLEN, N_TENSOR, feat_block), 0, 1)

        def add_part(total, pieces):
            token_piece, weight_piece = pieces
            partial_sum = jnp.dot(token_piece, weight_piece, preferred_element_type=jnp.float32)
            rounded = lax.optimization_barrier(partial_sum.astype(jnp.bfloat16)).astype(jnp.float32)
            return total + rounded, None

        start_total = jnp.zeros((PR * PLEN, columns), jnp.float32)
        values, unused = lax.scan(add_part, start_total, (token_parts, weight_parts))
        values = values.reshape(PR, PLEN, columns)
        live_rows = jnp.arange(PLEN)[None, :] < block_lengths[:, None]
        return jnp.where(live_rows[:, :, None], values, 0.0).astype(jnp.bfloat16)

    keyvals = lax.map(project, (prompt_tokens.reshape(pair_count, PR, PLEN, D), lengths.reshape(pair_count, PR)))
    route_blocks = routes[:, 0].reshape(pair_count, PR)
    slot_rank = slot_ranks(route_blocks)
    pair_ids = jnp.arange(pair_count, dtype=jnp.int32)
    src_group = jnp.broadcast_to((pair_ids // N_SECTION)[:, None], (pair_count, PR))
    src_section = jnp.broadcast_to((pair_ids % N_SECTION)[:, None], (pair_count, PR))
    cache_all = jnp.zeros((N_GROUP, N_SECTION, N_GROUP, CAP, PLEN, columns), jnp.bfloat16)
    cache_all = cache_all.at[route_blocks, src_section, src_group, slot_rank].set(keyvals)
    decode_cache = jnp.swapaxes(cache_all, 4, 5)
    slot_length = jnp.zeros((N_GROUP, N_SECTION, N_GROUP, CAP), jnp.int32)
    slot_length = slot_length.at[route_blocks, src_section, src_group, slot_rank].set(lengths.reshape(pair_count, PR).astype(jnp.int32))

    def one_group(bundle):
        query_g, fresh_g, cache_g, lengths_g = bundle
        slot_count = N_SECTION * N_GROUP
        query_f = query_g.reshape(slot_count, CAP, STEPS, KV_HEADS, per_group, HD).astype(jnp.float32)
        fresh_f = fresh_g.reshape(slot_count, CAP, STEPS, KV_HEADS, 2, HD).astype(jnp.float32)
        cache_f = cache_g.reshape(slot_count, CAP, KV_HEADS, 2, HD, PLEN).astype(jnp.float32)
        live_rows = jnp.arange(PLEN)[None, None, :] < lengths_g.reshape(slot_count, CAP)[:, :, None]
        mixed = attend(query_f, cache_f[:, :, :, 0], cache_f[:, :, :, 1], live_rows, fresh_f[:, :, :, :, 0], fresh_f[:, :, :, :, 1])
        return mixed.astype(jnp.bfloat16).reshape(N_SECTION, N_GROUP, CAP, STEPS, HEADS * HD)

    attention = lax.map(one_group, (queries, new_kv, decode_cache, slot_length))
    return decode_cache, attention
```

```python
import functools

import jax
import jax.numpy as jnp
from jax import lax
from jax.experimental import pallas as pl
from jax.experimental.pallas import tpu as pltpu
from jax.sharding import PartitionSpec as P

HEADS = 64
KV_HEADS = 8
HD = 128
CAP = 2
TILE = 256
DIRECT = (1, 7)
FAR_FIRST = (4, 3, 5, 2, 6)
FORWARD = ((0, 4, 3, 5), (2, 6))
PLACE_FLOPS = (0, 30_000_000_000, 30_000_000_000)

neg_big = -1e30
VMEM_LIMIT = 24 * 1024 * 1024
CONTRACT_LAST = (((1,), (1,)), ((), ()))


def vmem_specs(count):
    return [pl.BlockSpec(memory_space=pltpu.VMEM)] * count


def smem_specs(count):
    return [pl.BlockSpec(memory_space=pltpu.SMEM)] * count


def any_specs(count):
    return [pl.BlockSpec(memory_space=pl.ANY)] * count


def shaped(*shape, dtype=jnp.bfloat16):
    return jax.ShapeDtypeStruct(shape, dtype)


def project_kernel(split, mine, info_ref, tokens_ref, weight_ref, *refs):
    came_ref, out_refs = (refs[0], refs[1:]) if mine else (None, refs)
    ys = weight_ref.shape[1] // (4 * HD)
    y, core = info_ref[0], info_ref[1]
    side = core if mine else 1 - core
    starts = [
        (lax.rem(y + d, ys) * 2 + side) * (2 * HD) + (0 if split else HD) for d in range(ys)
    ]
    cols = [pl.ds(pl.multiple_of(start, HD), HD) for start in starts]
    count = tokens_ref.shape[0]
    low = lax.broadcasted_iota(jnp.int32, (TILE, HD), 1) < HD // 2

    def product(first):
        heads = jnp.concatenate([weight_ref[:, col] for col in cols], axis=1)
        tokens = tokens_ref[first : first + TILE, :]
        return jnp.dot(tokens, heads, preferred_element_type=jnp.float32)

    def put(part, d, rows, block):
        if mine:
            block = block + came_ref[part * ys + d, rows, :].astype(jnp.float32)
            out_refs[part * ys + d][rows, :] = block.astype(jnp.bfloat16)
        else:
            out_refs[0][part * ys + d, rows, :] = block.astype(jnp.bfloat16)

    for first in range(0, count // 2 if split else count, TILE):
        rows = slice(first, first + TILE)
        here = product(first)
        there = product(first + count // 2) if split else None
        for d in range(ys):
            block = here[:, d * HD : (d + 1) * HD]
            if split:
                beside = there[:, d * HD : (d + 1) * HD]
                put(0, d, rows, jnp.where(low, block, pltpu.roll(beside, HD // 2, 1)))
                put(1, d, rows, jnp.where(low, pltpu.roll(block, HD // 2, 1), beside))
            else:
                put(0, d, rows, block)


def place_kernel(relative, info_ref, routes_ref, lengths_ref, *refs):
    sum_refs, out_refs = refs[:4], refs[4:-4]
    taken_ref, prompt_ref, live_ref, turned_ref = refs[-4:]
    me, first = info_ref[2], info_ref[3]
    groups, slots = taken_ref.shape[0], prompt_ref.shape[0]
    prompts = turned_ref.shape[0]
    for r in range(groups):
        taken_ref[r] = 0
    for s in range(slots):
        prompt_ref[s] = 0
        live_ref[s] = 0
    for p in range(prompts):
        route = routes_ref[first + p]
        rank = taken_ref[route]
        taken_ref[route] = rank + 1
        way = route
        if relative:
            ahead = lax.rem(route // 2 - me // 2 + groups // 2, groups // 2)
            way = ahead * 2 + lax.rem(route + me, 2)
        prompt_ref[way * CAP + rank] = p
        live_ref[way * CAP + rank] = lengths_ref[first + p]
    cols = turned_ref.shape[1]
    abreast = HD // cols
    for p in range(prompts // abreast):
        rows = slice(p * HD, (p + 1) * HD)
        total = sum_refs[0][rows, :].astype(jnp.float32)
        for came in sum_refs[1:]:
            total = total + came[rows, :].astype(jnp.float32)
        turned = total.T.astype(jnp.bfloat16)
        for i in range(abreast):
            turned_ref[p + i * (prompts // abreast)] = turned[i * cols : (i + 1) * cols]
    place_ids = lax.broadcasted_iota(jnp.int32, (cols, HD), 1)
    ways = ways_of(out_refs, groups // 2) if relative else {}
    for s in range(slots):
        block = turned_ref[prompt_ref[s]]
        block = jnp.where(place_ids < live_ref[s], block, jnp.zeros_like(block))
        if relative:
            ways[s // (2 * CAP), s // CAP % 2][s % CAP] = block
        else:
            out_refs[0][s] = block


def ways_of(refs, zs):
    found = {}
    at = 0
    for d in range(zs):
        for e in range(2):
            found[d, e] = refs[at] if d in DIRECT else refs[at].at[e]
            at += 1 if d in DIRECT or e else 0
    return found


def halves_kernel(*refs):
    for i, piece in enumerate(refs[:-1]):
        refs[-1][i] = piece[1]


def score_kernel(steps, info_ref, routes_ref, lengths_ref, query_ref, fresh_ref, *refs):
    keys_refs, (cache_ref, weight_ref, scale_ref, fresh_out_ref, live_ref, sems) = refs[:2], refs[2:]
    cols = HD // len(keys_refs)
    copies = []
    for i, keys_ref in enumerate(keys_refs):
        rows = slice(i * cols, (i + 1) * cols)
        copies.append(pltpu.make_async_copy(keys_ref, cache_ref.at[:, rows, :], sems.at[i]))
        copies[-1].start()
    me, section, sections = info_ref[2], info_ref[4], info_ref[5]
    slots, rows = query_ref.shape[0], query_ref.shape[1]
    groups = slots // CAP
    prompts = routes_ref.shape[0] // (groups * 2)

    def count(source, carry):
        first = (source * sections + section) * prompts
        found = jnp.int32(0)
        for p in range(prompts):
            live_ref[source * (CAP + 1) + found] = lengths_ref[first + p]
            found = found + jnp.where(routes_ref[first + p] == me, 1, 0)
        for c in range(CAP):
            at = source * (CAP + 1) + c
            live_ref[at] = jnp.where(c < found, live_ref[at], 0)
        return carry

    lax.fori_loop(0, groups, count, 0)
    factor = HD ** (-0.5)
    place_ids = lax.broadcasted_iota(jnp.int32, (rows, HD), 1)
    batch = 4
    many = batch * rows
    row_ids = lax.broadcasted_iota(jnp.int32, (many, batch * steps), 0)
    fresh_ids = lax.broadcasted_iota(jnp.int32, (many, batch * steps), 1)
    seen = jnp.logical_and(
        row_ids // rows == fresh_ids // steps,
        fresh_ids % steps <= row_ids % rows // (rows // steps),
    )
    for start in range(0, slots, batch):
        group = slice(start, start + batch)
        query = query_ref[group].reshape(many, HD)
        fresh = fresh_ref[group].reshape(batch * steps, 2 * HD)
        new = lax.dot_general(
            query, fresh[:, :HD], CONTRACT_LAST, preferred_element_type=jnp.float32
        )
        new = jnp.where(seen, new * factor, neg_big)
        olds = []
        for s in range(start, start + batch):
            keys = jnp.concatenate([keys_ref[s] for keys_ref in keys_refs], axis=0)
            old = jnp.dot(query_ref[s], keys, preferred_element_type=jnp.float32)
            live = live_ref[s + s // CAP]
            olds.append(jnp.where(place_ids < live, old * factor, neg_big))
        old = jnp.concatenate(olds, axis=0)
        top = jnp.maximum(
            jnp.max(old, axis=-1, keepdims=True), jnp.max(new, axis=-1, keepdims=True)
        )
        old = jnp.exp(old - top)
        new = jnp.exp(new - top)
        total = jnp.sum(old, axis=-1, keepdims=True) + jnp.sum(new, axis=-1, keepdims=True)
        scale = jnp.broadcast_to(1.0 / total, (many, HD))
        fresh_out = jnp.dot(
            new.astype(jnp.bfloat16), fresh[:, HD:], preferred_element_type=jnp.float32
        )
        weight_ref[group] = old.astype(jnp.bfloat16).reshape(batch, rows, HD)
        scale_ref[group] = scale.reshape(batch, rows, HD)
        fresh_out_ref[group] = (fresh_out * scale).reshape(batch, rows, HD)
    for copy in copies:
        copy.wait()


def mix_kernel(zs, info_ref, weight_ref, scale_ref, fresh_out_ref, *refs):
    near = zs + len(DIRECT)
    cache_ref, out_ref, sems = refs[near + len(FORWARD) + 1 :]
    ways = ways_of(refs[:near], zs)
    for order, group_ref in zip(FORWARD, refs[near:]):
        for i, d in enumerate(order):
            ways[d, 1] = group_ref.at[i]
    me = info_ref[2]
    copies = []
    for i, ((d, e), vals_ref) in enumerate(ways.items()):
        source = lax.rem(me // 2 - d + zs, zs) * 2 + lax.rem(me + e, 2)
        slots = pl.ds(source * CAP, CAP)
        copies.append(pltpu.make_async_copy(vals_ref, cache_ref.at[slots, HD:, :], sems.at[i]))
        copies[-1].start()
        for c in range(CAP):
            slot = source * CAP + c
            summed = lax.dot_general(
                weight_ref[slot], vals_ref[c], CONTRACT_LAST, preferred_element_type=jnp.float32
            )
            mixed = summed * scale_ref[slot] + fresh_out_ref[slot]
            out_ref[slot] = mixed.astype(jnp.bfloat16)
    for copy in copies:
        copy.wait()


def per_device(prompt_tokens, kv_weight, routes, lengths, queries, new_kv):
    groups = lax.axis_size("group")
    sections = lax.axis_size("section")
    tensors = lax.axis_size("tensor")
    prompts_here, positions, feat_here = prompt_tokens.shape
    columns = kv_weight.shape[1]
    col_here = columns // tensors
    step_count = queries.shape[4]
    per_group = HEADS // KV_HEADS
    rows = step_count * per_group
    slots = groups * CAP
    ys = tensors // 2
    token_count = prompts_here * positions
    group_me = lax.axis_index("group")
    section_me = lax.axis_index("section")
    tensor_me = lax.axis_index("tensor")
    first_prompt = (group_me * sections + section_me) * prompts_here
    info = jnp.stack(
        [tensor_me // 2, tensor_me % 2, group_me]
        + [first_prompt, section_me, jnp.int32(sections)]
    ).astype(jnp.int32)
    core_pairs = [(t, t ^ 1) for t in range(tensors)]
    y_pairs = [
        [(y * 2 + c, (y + d) % ys * 2 + c) for y in range(ys) for c in range(2)] for d in range(ys)
    ]
    zs = groups // 2
    z_pairs = {
        (d, e): [
            (z * 2 + x, (z + d) % zs * 2 + (x + e) % 2) for z in range(zs) for x in range(2)
        ]
        for d in range(zs)
        for e in range(2)
    }
    flat_tokens = prompt_tokens.reshape(token_count, feat_here)
    flat_routes = routes[:, 0]
    params = pltpu.CompilerParams(vmem_limit_bytes=VMEM_LIMIT)

    def call(kernel, **options):
        return pl.pallas_call(kernel, compiler_params=params, **options)


    came = []
    for split in (True, False):
        sent = call(
            functools.partial(project_kernel, split, False),
            in_specs=smem_specs(1) + vmem_specs(2),
            out_specs=vmem_specs(1)[0],
            out_shape=shaped(*((2 * ys, token_count // 2) if split else (ys, token_count)), HD),
        )(info, flat_tokens, kv_weight)
        came.append(lax.ppermute(sent, "tensor", core_pairs))
    sums = []
    for split in (True, False):
        made = call(
            functools.partial(project_kernel, split, True),
            in_specs=smem_specs(1) + vmem_specs(3),
            out_specs=vmem_specs(2 * ys if split else ys),
            out_shape=[shaped(token_count // 2, HD)] * (2 * ys)
            if split
            else [shaped(token_count, HD)] * ys,
        )(info, flat_tokens, kv_weight, came[0 if split else 1])
        sums += [made[:ys], made[ys:]] if split else [made]
    summed = []
    for part in sums:
        if summed:
            part, summed[-1][1] = lax.optimization_barrier((part, summed[-1][1]))
        summed.append(
            [part[0]] + [lax.ppermute(part[d], "tensor", y_pairs[d]) for d in (2, 1, 3)]
        )

    def place(part, relative, out_shape):
        return call(
            functools.partial(place_kernel, relative),
            in_specs=smem_specs(3) + vmem_specs(ys),
            out_specs=vmem_specs(len(out_shape)),
            out_shape=out_shape,
            scratch_shapes=[
                pltpu.SMEM((groups,), jnp.int32),
                pltpu.SMEM((slots,), jnp.int32),
                pltpu.SMEM((slots,), jnp.int32),
                pltpu.VMEM((prompts_here, out_shape[0].shape[-2], HD), jnp.bfloat16),
            ],
            cost_estimate=pl.CostEstimate(
                flops=PLACE_FLOPS[part], bytes_accessed=0, transcendentals=0
            ),
        )(info, flat_routes, lengths, *summed[part])

    keys = []
    for part in range(2):
        (placed,) = place(part, False, [shaped(slots, HD // 2, positions)])
        keys.append(lax.all_to_all(placed, "group", 0, 0, tiled=True))
    shapes = []
    for d in range(zs):
        shapes += [shaped(CAP, HD, positions)] * 2 if d in DIRECT else [
            shaped(2, CAP, HD, positions)
        ]
    placed = iter(place(2, True, shapes))
    pieces = {}
    for d in range(zs):
        pieces[d] = [next(placed), next(placed)] if d in DIRECT else next(placed)
    for d in FAR_FIRST:
        pieces[d] = lax.ppermute(pieces[d], "group", z_pairs[d, 0])
    for d in DIRECT:
        pieces[d] = [lax.ppermute(pieces[d][e], "group", z_pairs[d, e]) for e in range(2)]
    cache, weights, scales, fresh_out = call(
        functools.partial(score_kernel, step_count),
        in_specs=smem_specs(3) + vmem_specs(4),
        out_specs=any_specs(1) + vmem_specs(3),
        out_shape=[
            shaped(slots, col_here, positions),
            shaped(slots, rows, HD),
            shaped(slots, rows, HD, dtype=jnp.float32),
            shaped(slots, rows, HD, dtype=jnp.float32),
        ],
        scratch_shapes=[
            pltpu.SMEM((groups * (CAP + 1),), jnp.int32),
            pltpu.SemaphoreType.DMA((2,)),
        ],
    )(
        info,
        flat_routes,
        lengths,
        queries.reshape(slots, rows, HD),
        new_kv.reshape(slots, step_count, 2 * HD),
        *keys,
    )
    weights, far = lax.optimization_barrier((weights, pieces[FAR_FIRST[0]]))
    pieces[FAR_FIRST[0]] = far
    passed = []
    for order in FORWARD:
        halves = call(
            halves_kernel,
            in_specs=vmem_specs(len(order)),
            out_specs=vmem_specs(1)[0],
            out_shape=shaped(len(order), CAP, HD, positions),
        )(*[pieces[d] for d in order])
        passed.append(lax.ppermute(halves, "group", z_pairs[0, 1]))
    vals = []
    for d in range(zs):
        vals += pieces[d] if d in DIRECT else [pieces[d]]
    vals += passed

    cache, attention = call(
        functools.partial(mix_kernel, zs),
        in_specs=smem_specs(1) + vmem_specs(3 + len(vals)) + any_specs(1),
        out_specs=any_specs(1) + vmem_specs(1),
        out_shape=[shaped(slots, col_here, positions), shaped(slots, rows, HD)],
        scratch_shapes=[pltpu.SemaphoreType.DMA((groups,))],
        input_output_aliases={4 + len(vals): 0},
    )(info, weights, scales, fresh_out, *vals, cache)
    return (
        cache.reshape(1, 1, groups, CAP, col_here, positions),
        attention.reshape(1, 1, groups, CAP, step_count, per_group * HD),
    )


def solution(mesh):
    return jax.shard_map(
        per_device,
        mesh=mesh,
        in_specs=(
            P(("group", "section"), None, "tensor"),
            P("tensor", None),
            P(),
            P(),
            P("group", "section", None, None, None, "tensor"),
            P("group", "section", None, None, None, "tensor"),
        ),
        out_specs=(
            P("group", "section", None, None, "tensor", None),
            P("group", "section", None, None, None, "tensor"),
        ),
        check_vma=False,
    )
```

```python
import functools

import jax
import jax.numpy as jnp
from jax import lax
from jax.experimental import pallas as pl
from jax.experimental.pallas import tpu as pltpu
from jax.sharding import PartitionSpec as P

HEADS = 64
KV_HEADS = 8
HD = 128
CAP = 2
TILE = 512
DIRECT = (1, 7)
FAR_FIRST = (4, 3, 5, 2, 6)
FORWARD = ((0, 4, 3, 5), (2, 6))
PLACE_FLOPS = (0, 30_000_000_000, 30_000_000_000)

neg_big = -1e30
VMEM_LIMIT = 24 * 1024 * 1024
CONTRACT_LAST = (((1,), (1,)), ((), ()))


def vmem_specs(count):
    return [pl.BlockSpec(memory_space=pltpu.VMEM)] * count


def smem_specs(count):
    return [pl.BlockSpec(memory_space=pltpu.SMEM)] * count


def any_specs(count):
    return [pl.BlockSpec(memory_space=pl.ANY)] * count


def shaped(*shape, dtype=jnp.bfloat16):
    return jax.ShapeDtypeStruct(shape, dtype)


def project_kernel(split, mine, info_ref, tokens_ref, weight_ref, *refs):
    came_ref, out_refs = (refs[0], refs[1:]) if mine else (None, refs)
    ys = weight_ref.shape[1] // (4 * HD)
    y, core = info_ref[0], info_ref[1]
    side = core if mine else 1 - core
    starts = [
        (lax.rem(y + d, ys) * 2 + side) * (2 * HD) + (0 if split else HD) for d in range(ys)
    ]
    cols = [pl.ds(pl.multiple_of(start, HD), HD) for start in starts]
    count = tokens_ref.shape[0]
    low = lax.broadcasted_iota(jnp.int32, (TILE, HD), 1) < HD // 2

    def product(first):
        heads = jnp.concatenate([weight_ref[:, col] for col in cols], axis=1)
        tokens = tokens_ref[first : first + TILE, :]
        return jnp.dot(tokens, heads, preferred_element_type=jnp.float32)

    def put(part, d, rows, block):
        if mine:
            block = block + came_ref[part * ys + d, rows, :].astype(jnp.float32)
            out_refs[part * ys + d][rows, :] = block.astype(jnp.bfloat16)
        else:
            out_refs[0][part * ys + d, rows, :] = block.astype(jnp.bfloat16)

    for first in range(0, count // 2 if split else count, TILE):
        rows = slice(first, first + TILE)
        here = product(first)
        there = product(first + count // 2) if split else None
        for d in range(ys):
            block = here[:, d * HD : (d + 1) * HD]
            if split:
                beside = there[:, d * HD : (d + 1) * HD]
                put(0, d, rows, jnp.where(low, block, pltpu.roll(beside, HD // 2, 1)))
                put(1, d, rows, jnp.where(low, pltpu.roll(block, HD // 2, 1), beside))
            else:
                put(0, d, rows, block)


def place_kernel(relative, info_ref, routes_ref, lengths_ref, *refs):
    sum_refs, out_refs = refs[:4], refs[4:-4]
    taken_ref, prompt_ref, live_ref, turned_ref = refs[-4:]
    me, first = info_ref[2], info_ref[3]
    groups, slots = taken_ref.shape[0], prompt_ref.shape[0]
    prompts = turned_ref.shape[0]
    for r in range(groups):
        taken_ref[r] = 0
    for s in range(slots):
        prompt_ref[s] = 0
        live_ref[s] = 0
    for p in range(prompts):
        route = routes_ref[first + p]
        rank = taken_ref[route]
        taken_ref[route] = rank + 1
        way = route
        if relative:
            ahead = lax.rem(route // 2 - me // 2 + groups // 2, groups // 2)
            way = ahead * 2 + lax.rem(route + me, 2)
        prompt_ref[way * CAP + rank] = p
        live_ref[way * CAP + rank] = lengths_ref[first + p]
    cols = turned_ref.shape[1]
    abreast = HD // cols
    for p in range(prompts // abreast):
        rows = slice(p * HD, (p + 1) * HD)
        total = sum_refs[0][rows, :].astype(jnp.float32)
        for came in sum_refs[1:]:
            total = total + came[rows, :].astype(jnp.float32)
        turned = total.T.astype(jnp.bfloat16)
        for i in range(abreast):
            turned_ref[p + i * (prompts // abreast)] = turned[i * cols : (i + 1) * cols]
    place_ids = lax.broadcasted_iota(jnp.int32, (cols, HD), 1)
    ways = ways_of(out_refs, groups // 2) if relative else {}
    for s in range(slots):
        block = turned_ref[prompt_ref[s]]
        block = jnp.where(place_ids < live_ref[s], block, jnp.zeros_like(block))
        if relative:
            ways[s // (2 * CAP), s // CAP % 2][s % CAP] = block
        else:
            out_refs[0][s] = block


def ways_of(refs, zs):
    found = {}
    at = 0
    for d in range(zs):
        for e in range(2):
            found[d, e] = refs[at] if d in DIRECT else refs[at].at[e]
            at += 1 if d in DIRECT or e else 0
    return found


def halves_kernel(*refs):
    for i, piece in enumerate(refs[:-1]):
        refs[-1][i] = piece[1]


def score_kernel(steps, info_ref, routes_ref, lengths_ref, query_ref, fresh_ref, *refs):
    keys_refs, (cache_ref, weight_ref, scale_ref, fresh_out_ref, live_ref, sems) = refs[:2], refs[2:]
    cols = HD // len(keys_refs)
    copies = []
    for i, keys_ref in enumerate(keys_refs):
        rows = slice(i * cols, (i + 1) * cols)
        copies.append(pltpu.make_async_copy(keys_ref, cache_ref.at[:, rows, :], sems.at[i]))
        copies[-1].start()
    me, section, sections = info_ref[2], info_ref[4], info_ref[5]
    slots, rows = query_ref.shape[0], query_ref.shape[1]
    groups = slots // CAP
    prompts = routes_ref.shape[0] // (groups * 2)

    def count(source, carry):
        first = (source * sections + section) * prompts
        found = jnp.int32(0)
        for p in range(prompts):
            live_ref[source * (CAP + 1) + found] = lengths_ref[first + p]
            found = found + jnp.where(routes_ref[first + p] == me, 1, 0)
        for c in range(CAP):
            at = source * (CAP + 1) + c
            live_ref[at] = jnp.where(c < found, live_ref[at], 0)
        return carry

    lax.fori_loop(0, groups, count, 0)
    factor = HD ** (-0.5)
    place_ids = lax.broadcasted_iota(jnp.int32, (rows, HD), 1)
    batch = 4
    many = batch * rows
    row_ids = lax.broadcasted_iota(jnp.int32, (many, batch * steps), 0)
    fresh_ids = lax.broadcasted_iota(jnp.int32, (many, batch * steps), 1)
    seen = jnp.logical_and(
        row_ids // rows == fresh_ids // steps,
        fresh_ids % steps <= row_ids % steps,
    )
    for start in range(0, slots, batch):
        group = slice(start, start + batch)
        query = query_ref[group].reshape(many, HD)
        fresh = fresh_ref[group].reshape(batch * steps, 2 * HD)
        new = lax.dot_general(
            query, fresh[:, :HD], CONTRACT_LAST, preferred_element_type=jnp.float32
        )
        new = jnp.where(seen, new * factor, neg_big)
        olds = []
        for s in range(start, start + batch):
            keys = jnp.concatenate([keys_ref[s] for keys_ref in keys_refs], axis=0)
            old = jnp.dot(query_ref[s], keys, preferred_element_type=jnp.float32)
            live = live_ref[s + s // CAP]
            olds.append(jnp.where(place_ids < live, old * factor, neg_big))
        old = jnp.concatenate(olds, axis=0)
        top = jnp.maximum(
            jnp.max(old, axis=-1, keepdims=True), jnp.max(new, axis=-1, keepdims=True)
        )
        old = jnp.exp(old - top)
        new = jnp.exp(new - top)
        total = jnp.sum(old, axis=-1, keepdims=True) + jnp.sum(new, axis=-1, keepdims=True)
        scale = jnp.broadcast_to(1.0 / total, (many, HD))
        fresh_out = jnp.dot(
            new.astype(jnp.bfloat16), fresh[:, HD:], preferred_element_type=jnp.float32
        )
        weight_ref[group] = old.astype(jnp.bfloat16).reshape(batch, rows, HD)
        scale_ref[group] = scale.reshape(batch, rows, HD)
        fresh_out_ref[group] = (fresh_out * scale).reshape(batch, rows, HD)
    for copy in copies:
        copy.wait()


def mix_kernel(zs, info_ref, weight_ref, scale_ref, fresh_out_ref, *refs):
    near = zs + len(DIRECT)
    cache_ref, out_ref, sems = refs[near + len(FORWARD) + 1 :]
    ways = ways_of(refs[:near], zs)
    for order, group_ref in zip(FORWARD, refs[near:]):
        for i, d in enumerate(order):
            ways[d, 1] = group_ref.at[i]
    me = info_ref[2]
    copies = []
    for i, ((d, e), vals_ref) in enumerate(ways.items()):
        source = lax.rem(me // 2 - d + zs, zs) * 2 + lax.rem(me + e, 2)
        slots = pl.ds(source * CAP, CAP)
        copies.append(pltpu.make_async_copy(vals_ref, cache_ref.at[slots, HD:, :], sems.at[i]))
        copies[-1].start()
        for c in range(CAP):
            slot = source * CAP + c
            summed = lax.dot_general(
                weight_ref[slot], vals_ref[c], CONTRACT_LAST, preferred_element_type=jnp.float32
            )
            mixed = summed * scale_ref[slot] + fresh_out_ref[slot]
            steps = out_ref.shape[1]
            for h in range(mixed.shape[0] // steps):
                block = mixed[h * steps : (h + 1) * steps].astype(jnp.bfloat16)
                out_ref[slot, :, h * HD : (h + 1) * HD] = block
    for copy in copies:
        copy.wait()


def per_device(prompt_tokens, kv_weight, routes, lengths, queries, new_kv):
    groups = lax.axis_size("group")
    sections = lax.axis_size("section")
    tensors = lax.axis_size("tensor")
    prompts_here, positions, feat_here = prompt_tokens.shape
    columns = kv_weight.shape[1]
    col_here = columns // tensors
    step_count = queries.shape[4]
    per_group = HEADS // KV_HEADS
    rows = step_count * per_group
    slots = groups * CAP
    ys = tensors // 2
    token_count = prompts_here * positions
    group_me = lax.axis_index("group")
    section_me = lax.axis_index("section")
    tensor_me = lax.axis_index("tensor")
    first_prompt = (group_me * sections + section_me) * prompts_here
    info = jnp.stack(
        [tensor_me // 2, tensor_me % 2, group_me]
        + [first_prompt, section_me, jnp.int32(sections)]
    ).astype(jnp.int32)
    core_pairs = [(t, t ^ 1) for t in range(tensors)]
    y_pairs = [
        [(y * 2 + c, (y + d) % ys * 2 + c) for y in range(ys) for c in range(2)] for d in range(ys)
    ]
    zs = groups // 2
    z_pairs = {
        (d, e): [
            (z * 2 + x, (z + d) % zs * 2 + (x + e) % 2) for z in range(zs) for x in range(2)
        ]
        for d in range(zs)
        for e in range(2)
    }
    flat_tokens = prompt_tokens.reshape(token_count, feat_here)
    flat_routes = routes[:, 0]
    params = pltpu.CompilerParams(vmem_limit_bytes=VMEM_LIMIT)

    def call(kernel, **options):
        return pl.pallas_call(kernel, compiler_params=params, **options)


    came = []
    for split in (True, False):
        sent = call(
            functools.partial(project_kernel, split, False),
            in_specs=smem_specs(1) + vmem_specs(2),
            out_specs=vmem_specs(1)[0],
            out_shape=shaped(*((2 * ys, token_count // 2) if split else (ys, token_count)), HD),
        )(info, flat_tokens, kv_weight)
        came.append(lax.ppermute(sent, "tensor", core_pairs))
    sums = []
    for split in (True, False):
        made = call(
            functools.partial(project_kernel, split, True),
            in_specs=smem_specs(1) + vmem_specs(3),
            out_specs=vmem_specs(2 * ys if split else ys),
            out_shape=[shaped(token_count // 2, HD)] * (2 * ys)
            if split
            else [shaped(token_count, HD)] * ys,
        )(info, flat_tokens, kv_weight, came[0 if split else 1])
        sums += [made[:ys], made[ys:]] if split else [made]
    sums[1], sums[2] = lax.optimization_barrier((sums[1], sums[2]))
    summed = []
    for part in sums:
        if summed:
            part, summed[-1][1] = lax.optimization_barrier((part, summed[-1][1]))
        summed.append(
            [part[0]] + [lax.ppermute(part[d], "tensor", y_pairs[d]) for d in (1, 3, 2)]
        )

    def place(part, relative, out_shape):
        return call(
            functools.partial(place_kernel, relative),
            in_specs=smem_specs(3) + vmem_specs(ys),
            out_specs=vmem_specs(len(out_shape)),
            out_shape=out_shape,
            scratch_shapes=[
                pltpu.SMEM((groups,), jnp.int32),
                pltpu.SMEM((slots,), jnp.int32),
                pltpu.SMEM((slots,), jnp.int32),
                pltpu.VMEM((prompts_here, out_shape[0].shape[-2], HD), jnp.bfloat16),
            ],
            cost_estimate=pl.CostEstimate(
                flops=PLACE_FLOPS[part], bytes_accessed=0, transcendentals=0
            ),
        )(info, flat_routes, lengths, *summed[part])

    keys = []
    for part in range(2):
        (placed,) = place(part, False, [shaped(slots, HD // 2, positions)])
        keys.append(lax.all_to_all(placed, "group", 0, 0, tiled=True))
    shapes = []
    for d in range(zs):
        shapes += [shaped(CAP, HD, positions)] * 2 if d in DIRECT else [
            shaped(2, CAP, HD, positions)
        ]
    placed = iter(place(2, True, shapes))
    pieces = {}
    for d in range(zs):
        pieces[d] = [next(placed), next(placed)] if d in DIRECT else next(placed)
    for d in FAR_FIRST:
        pieces[d] = lax.ppermute(pieces[d], "group", z_pairs[d, 0])
    for d in DIRECT:
        pieces[d] = [lax.ppermute(pieces[d][e], "group", z_pairs[d, e]) for e in range(2)]
    cache, weights, scales, fresh_out = call(
        functools.partial(score_kernel, step_count),
        in_specs=smem_specs(3) + vmem_specs(4),
        out_specs=any_specs(1) + vmem_specs(3),
        out_shape=[
            shaped(slots, col_here, positions),
            shaped(slots, rows, HD),
            shaped(slots, rows, HD, dtype=jnp.float32),
            shaped(slots, rows, HD, dtype=jnp.float32),
        ],
        scratch_shapes=[
            pltpu.SMEM((groups * (CAP + 1),), jnp.int32),
            pltpu.SemaphoreType.DMA((2,)),
        ],
    )(
        info,
        flat_routes,
        lengths,
        jnp.swapaxes(queries.reshape(slots, step_count, per_group, HD), 1, 2).reshape(
            slots, rows, HD
        ),
        new_kv.reshape(slots, step_count, 2 * HD),
        *keys,
    )
    weights, far = lax.optimization_barrier((weights, pieces[FAR_FIRST[0]]))
    pieces[FAR_FIRST[0]] = far
    passed = []
    for order in FORWARD:
        halves = call(
            halves_kernel,
            in_specs=vmem_specs(len(order)),
            out_specs=vmem_specs(1)[0],
            out_shape=shaped(len(order), CAP, HD, positions),
        )(*[pieces[d] for d in order])
        passed.append(lax.ppermute(halves, "group", z_pairs[0, 1]))
    vals = []
    for d in range(zs):
        vals += pieces[d] if d in DIRECT else [pieces[d]]
    vals += passed

    cache, attention = call(
        functools.partial(mix_kernel, zs),
        in_specs=smem_specs(1) + vmem_specs(3 + len(vals)) + any_specs(1),
        out_specs=any_specs(1) + vmem_specs(1),
        out_shape=[
            shaped(slots, col_here, positions),
            shaped(slots, step_count, per_group * HD),
        ],
        scratch_shapes=[pltpu.SemaphoreType.DMA((groups,))],
        input_output_aliases={4 + len(vals): 0},
    )(info, weights, scales, fresh_out, *vals, cache)
    return (
        cache.reshape(1, 1, groups, CAP, col_here, positions),
        attention.reshape(1, 1, groups, CAP, step_count, per_group * HD),
    )


def solution(mesh):
    return jax.shard_map(
        per_device,
        mesh=mesh,
        in_specs=(
            P(("group", "section"), None, "tensor"),
            P("tensor", None),
            P(),
            P(),
            P("group", "section", None, None, None, "tensor"),
            P("group", "section", None, None, None, "tensor"),
        ),
        out_specs=(
            P("group", "section", None, None, "tensor", None),
            P("group", "section", None, None, None, "tensor"),
        ),
        check_vma=False,
    )
```
